128 devices in a mesh: grp: 16 (over y, x), tp: 8 (over z, core).
Axes of the slice: x: 4, y: 4, z: 4, core: 2. Of those that a mesh axis runs over, the one named last changes fastest.
Arguments:
- prompt_len: int32 [256], replicated, may hold values from 1 to 1022, 131072 in all
- request_owner: int32 [16, 16], replicated, may hold values from 0 to 15, each once within a row
- page_table: int32 [16, 128], P('grp'), may hold values from 0 to 127, each once within a row
- kv_pool: bfloat16 [2048, 2, 8, 128, 128], P('grp', None, 'tp'), may hold values from -400 to 400
- step_input: bfloat16 [2, 256, 8192], P(None, None, 'grp'), may hold values from -250 to 250
- norm_gain: bfloat16 [8192], P('grp'), may hold values from 0.5 to 1.5
- w_qkv: bfloat16 [8192, 8, 1280], P('grp', 'tp'), may hold values from -1 to 1
- w_out: bfloat16 [8, 1024, 8192], P('tp', None, 'grp'), may hold values from -0.375 to 0.375
Outputs:
- attn_out: bfloat16 [2, 256, 8192], P(None, None, 'grp')
- decode_cache: bfloat16 [256, 8, 2, 8, 128, 128], P('grp', None, None, 'tp')
The draws below stay inside these ranges and needn't reach their ends.
Inputs may be any that keep to these rules, and one draw needn't show every extreme that they name: `request_owner`: each row names every decode group once: each prefill shard hands one request to each group. `page_table`: each row holds each page slot of its prefill shard once; slot j of the shard keeps its page p at entry j * 8 + p.
All inputs are finite; a program needn't handle non-finite values.
Results may differ from the reference program's by a relative error of at most 0.005.
The reference program's roundings to bfloat16 on the way count: a program that leaves them out, or rounds other values in their place, can miss the bound.
Values may be sent and summed in bfloat16 or wider, within the bound.
No kernel may reach another device: no remote copies, remote signals or barrier semaphores. Data moves between devices by JAX's collectives and lax.ppermute only.
A program may use at most 128 MiB of HBM per device.

```python
import math
import jax
import jax.numpy as jnp
import numpy as np
from jax import lax

D = 8192
HEADS = 64
KVH = 8
HD = 128
PAGE = 128
MAXP = 8
STEPS = 2
G = 8
REQUESTS = 256
POOL = 2048
N_GRP = 16


def draw_step_input(key, part):
    key = jax.random.fold_in(key, 11)
    first_key, second_key, third_key = jax.random.split(key, 3)
    full_shape = (STEPS, REQUESTS, D)
    row_scale = jnp.exp(jax.random.uniform(second_key, (STEPS, REQUESTS, 1)) * math.log(10.0))
    rising = jnp.exp(jnp.arange(D, dtype=jnp.float32) / D * math.log(3.0))
    column_scale = jnp.exp(jax.random.uniform(third_key, (D,)) * math.log(10.0)) * rising
    sample = jax.random.normal(first_key, full_shape)
    sample = jnp.clip(sample, -5.0, 5.0)
    return (sample * row_scale * column_scale[None, None, :] / 10.0).astype(jnp.bfloat16)


def draw_kv_pool(key, part):
    key = jax.random.fold_in(key, 23)
    first_key = jax.random.fold_in(key, 0)
    full_shape = (POOL, 2, KVH, PAGE, HD)
    sample = jnp.clip(jax.random.normal(first_key, full_shape), -5.0, 5.0)
    return sample.astype(jnp.bfloat16)


def draw_w_qkv(key, part):
    key = jax.random.fold_in(key, 37)
    first_key, second_key = jax.random.split(key, 2)
    group_heads = HEADS // KVH
    full_shape = (D, KVH, (group_heads + 2) * HD)
    sample = jnp.clip(jax.random.normal(first_key, full_shape), -5.0, 5.0)
    sample = sample / math.sqrt(D)
    tie_level = jnp.exp(jax.random.uniform(second_key, (1, KVH, group_heads, 1), minval=math.log(0.35), maxval=math.log(0.6)))
    query_part = sample[:, :, :group_heads * HD].reshape(D, KVH, group_heads, HD)
    key_part = sample[:, :, group_heads * HD:(group_heads + 1) * HD]
    query_part = tie_level * key_part[:, :, None, :] + jnp.sqrt(1.0 - tie_level * tie_level) * query_part
    merged = jnp.concatenate([query_part.reshape(D, KVH, group_heads * HD), sample[:, :, group_heads * HD:]], axis=-1)
    return merged.astype(jnp.bfloat16)


def block_levels(stream_key, shape, cuts, low, top_value):
    def one(axis_at, shards_of):
        draws = jax.random.uniform(jax.random.fold_in(jax.random.fold_in(stream_key, 6), axis_at), (shards_of,), jnp.float32, low / len(cuts), top_value / len(cuts))
        return jnp.repeat(jnp.exp(draws), shape[axis_at] // shards_of).reshape((-1,) + (1,) * (len(shape) - axis_at - 1))

    gain = one(*cuts[0])
    for cut in cuts[1:]:
        gain = gain * one(*cut)
    return gain


def profile(amount, total, limit, slope):
    portions = [(1 << 20) // math.isqrt(rank ** slope) + 1 for rank in range(2, amount + 1)]
    rest, counts = total - limit - (amount - 1), [1] * (amount - 1)
    while rest > 0:
        free = [i for i in range(amount - 1) if counts[i] < limit]
        whole, left = sum([portions[i] for i in free]), rest
        for i in free:
            extra = min(limit - counts[i], max(1, left * portions[i] // whole), rest)
            counts[i] = counts[i] + extra
            rest = rest - extra
    return np.array([limit] + counts)


def ragged(key, count, total, reach, skew):
    if count == 2:
        one = jax.random.randint(key, (), max(1, total - reach), min(reach, total - 1) + 1)
        return jnp.stack([one, total - one])
    sizes = jnp.asarray(profile(count, total, reach, skew), jnp.int32)
    twos = (count - 1) // 2
    giver, taker = sizes[1:1 + 2 * twos:2], sizes[2:2 + 2 * twos:2]
    room = jnp.minimum(giver - 1, reach - taker)
    moved = jax.random.randint(jax.random.fold_in(key, 1), (twos,), 0, 1 << 20) % (room + 1)
    sizes = sizes.at[1:1 + 2 * twos:2].set(giver - moved).at[2:2 + 2 * twos:2].set(taker + moved)
    return sizes[jax.random.permutation(jax.random.fold_in(key, 2), count)]


def gaussian(rng, shape, deviation, limit, cuts=(), kind=jnp.bfloat16):
    result = jax.random.normal(rng, shape, jnp.float32) * deviation
    if len(cuts) > 0:
        result = block_levels(rng, shape, cuts, -0.22, 0.18) * result
    return jnp.clip(result, min=-limit, max=limit).astype(kind)


def setup_inputs(seed: int = 0) -> dict:
    seeds = jax.random.split(jax.random.key(seed), 9)
    return {
        "prompt_len": ragged(seeds[0], REQUESTS, REQUESTS * MAXP * PAGE // 2, MAXP * PAGE - 2, 2).astype(jnp.int32),
        "request_owner": jax.vmap(lambda own: jax.random.permutation(own, N_GRP))(jax.random.split(seeds[1], N_GRP)).reshape((N_GRP, N_GRP)).astype(jnp.int32),
        "page_table": jax.vmap(lambda own: jax.random.permutation(own, N_GRP * MAXP))(jax.random.split(seeds[2], N_GRP)).reshape((N_GRP, N_GRP * MAXP)).astype(jnp.int32),
        "kv_pool": draw_kv_pool(jax.random.fold_in(seeds[8], 71), 0),
        "step_input": draw_step_input(jax.random.fold_in(seeds[8], 71), 0),
        "norm_gain": jnp.clip(1.0 + 0.1 * jax.random.normal(seeds[5], (D,), jnp.float32), 0.5, 1.5).astype(jnp.bfloat16),
        "w_qkv": draw_w_qkv(jax.random.fold_in(seeds[8], 71), 0),
        "w_out": gaussian(seeds[7], (KVH, G * HD, D), (HEADS * HD // 32) ** -0.5, 0.375, ((0, 8), (2, 16))),
    }


epsilon = 1e-05
negative_big = -1e+30

def page_stats(queries, key_rows, value_rows, valid_mask):
    score_scale = 1.0 / math.sqrt(queries.shape[-1])
    scores = jnp.einsum('nskge,npkie->npskgi', queries.astype(jnp.float32), key_rows.astype(jnp.float32)) * score_scale
    allowed = valid_mask[:, :, :, None, None, :]
    top_score = lax.optimization_barrier(jnp.max(jnp.where(allowed, scores, negative_big), axis=-1))
    exponent = jnp.where(allowed, jnp.exp(scores - top_score[..., None]), 0.0)
    weight_sum = lax.optimization_barrier(jnp.sum(exponent, axis=-1))
    weighted = jnp.einsum('npskgi,npkie->npskge', exponent.astype(jnp.bfloat16).astype(jnp.float32), value_rows.astype(jnp.float32))
    return (top_score, weight_sum, weighted)

def fresh_block(queries, key_new, value_new):
    step_count = key_new.shape[1]
    key_rows = jnp.transpose(key_new, (0, 2, 1, 3))[:, None]
    value_rows = jnp.transpose(value_new, (0, 2, 1, 3))[:, None]
    step_ids = jnp.arange(step_count, dtype=jnp.int32)
    valid_mask = (step_ids[None, :] <= step_ids[:, None])[None, None]
    return page_stats(queries, key_rows, value_rows, valid_mask)

def combine(partials):
    top_score = jnp.concatenate([partial_stat[0] for partial_stat in partials], axis=1)
    weight_sum = jnp.concatenate([partial_stat[1] for partial_stat in partials], axis=1)
    weighted = jnp.concatenate([partial_stat[2] for partial_stat in partials], axis=1)
    best_score = lax.optimization_barrier(jnp.max(top_score, axis=1, keepdims=True))
    factor = jnp.exp(top_score - best_score)
    numerator = lax.optimization_barrier(jnp.sum(weighted * factor[..., None], axis=1))
    denominator = lax.optimization_barrier(jnp.sum(weight_sum * factor, axis=1))
    return (numerator / denominator[..., None]).astype(jnp.bfloat16)

def insert_tokens(page_data, lengths, key_new, value_new):
    page_count = page_data.shape[1]
    page_len = page_data.shape[4]
    step_count = key_new.shape[1]
    positions = jnp.arange(page_count * page_len, dtype=jnp.int32).reshape(page_count, page_len)
    target = lengths[:, None] + jnp.arange(step_count, dtype=jnp.int32)[None, :]
    new_marks = (positions[None, None] == target[:, :, None, None]).astype(jnp.float32)
    fresh_rows = jnp.stack((key_new, value_new), axis=2).astype(jnp.float32)
    new_tokens = jnp.einsum('nspi,nscke->npckie', new_marks, fresh_rows)
    return (page_data.astype(jnp.float32) + new_tokens).astype(jnp.bfloat16)

def reference(prompt_len, request_owner, page_table, kv_pool, step_input, norm_gain, w_qkv, w_out):
    groups = request_owner.shape[0]
    step_count = step_input.shape[0]
    group_heads = HEADS // KVH
    values_x = step_input.astype(jnp.float32)
    squares = lax.optimization_barrier(jnp.sum(values_x * values_x, axis=-1))
    inv_rms = lax.rsqrt(squares / D + epsilon)
    normed = (values_x * norm_gain.astype(jnp.float32)).astype(jnp.bfloat16)
    projected = jnp.einsum('srd,dkc->srkc', normed.astype(jnp.float32), w_qkv.astype(jnp.float32)) * inv_rms[:, :, None, None]
    queries = projected[..., :group_heads * HD].reshape(step_count, REQUESTS, KVH, group_heads, HD).astype(jnp.bfloat16)
    key_new = projected[..., group_heads * HD:(group_heads + 1) * HD].astype(jnp.bfloat16)
    value_new = projected[..., (group_heads + 1) * HD:].astype(jnp.bfloat16)
    slot_ids = jnp.arange(groups, dtype=jnp.int32)
    slot_of = lax.optimization_barrier(jnp.sum(slot_ids[None, :, None] * (request_owner[:, :, None] == slot_ids[None, None, :]), axis=1)).astype(jnp.int32)
    page_ids = page_table.reshape(groups, groups, MAXP)
    positions = jnp.arange(MAXP * PAGE, dtype=jnp.int32).reshape(MAXP, PAGE)

    def serve_owner(target):
        chosen = slot_of[:, target]
        requests = slot_ids * groups + chosen
        lengths = prompt_len[requests]
        pool_rows = slot_ids[:, None] * (groups * MAXP) + page_ids[slot_ids, chosen]
        page_data = kv_pool[pool_rows]
        valid_mask = positions[None] < lengths[:, None, None]
        page_data = jnp.where(valid_mask[:, :, None, None, :, None], page_data, jnp.zeros((), page_data.dtype))
        own_queries = jnp.transpose(queries[:, requests], (1, 0, 2, 3, 4))
        own_keys = jnp.transpose(key_new[:, requests], (1, 0, 2, 3))
        own_values = jnp.transpose(value_new[:, requests], (1, 0, 2, 3))
        cached = page_stats(own_queries, page_data[:, :, 0], page_data[:, :, 1], valid_mask[:, :, None, :])
        fresh_stats = fresh_block(own_queries, own_keys, own_values)
        attended = combine([cached, fresh_stats])
        return (attended, insert_tokens(page_data, lengths, own_keys, own_values))
    attended, decode_cache = lax.map(serve_owner, slot_ids)
    decode_cache = decode_cache.reshape(REQUESTS, MAXP, 2, KVH, PAGE, HD)
    back_order = (request_owner * groups + slot_ids[:, None]).reshape(-1)
    head_rows = attended.reshape(REQUESTS, step_count, HEADS * HD)[back_order]
    attn_out = jnp.einsum('rsf,fd->srd', head_rows.astype(jnp.float32), w_out.reshape(HEADS * HD, D).astype(jnp.float32)).astype(jnp.bfloat16)
    return (attn_out, decode_cache)
```

```python
import functools
import math

import jax
import jax.numpy as jnp
from jax import lax
from jax.experimental import pallas as pl
from jax.experimental.pallas import tpu as pltpu
from jax.sharding import PartitionSpec as P

D = 8192
PAGE = 128
HD = 128
MAXP = 8
STEPS = 2
TILE = 16
CORES = 2
SIDE = 4
SLOTS = 16
ROWS = STEPS * SLOTS
CUTS = (0, 4, 8)
OWNER, LENGTH, TABLE = 0, 256, 512

epsilon = 1e-05
negative_big = -1e30

HBM = pl.BlockSpec(memory_space=pltpu.HBM)
ANY = pl.BlockSpec(memory_space=pl.ANY)
SMEM = pl.BlockSpec(memory_space=pltpu.SMEM)
VMEM = pl.BlockSpec(memory_space=pltpu.VMEM)


def params(mib):
    return pltpu.CompilerParams(vmem_limit_bytes=mib * 2**20)


def cost(flops, moved):
    return pl.CostEstimate(flops=flops, bytes_accessed=moved, transcendentals=0)


def move_part(array, dz, dc):
    pairs = [(z * CORES + c, ((z + dz) % SIDE) * CORES + (c + dc) % CORES) for z in range(SIDE) for c in range(CORES)]
    return lax.ppermute(array, "tp", pairs)


def project_kernel(x_ref, gain_ref, w_ref, out_ref):
    shards = out_ref.shape[0]
    blocks = w_ref.shape[1] // HD
    gain = gain_ref[...].astype(jnp.float32)
    for st in range(STEPS):
        x = x_ref[st].astype(jnp.float32)
        squares = jnp.broadcast_to(jnp.sum(x * x, axis=-1, keepdims=True), (x.shape[0], HD))
        acc = jnp.dot((x * gain).astype(jnp.bfloat16), w_ref[...], preferred_element_type=jnp.float32)
        for c in range(blocks):
            out_ref[:, pl.ds(c * ROWS + st * SLOTS, SLOTS), :] = acc[:, c * HD:(c + 1) * HD].reshape(shards, SLOTS, HD)
        half = 8 // STEPS
        per = HD // SLOTS
        for t in range(x.shape[0] // HD):
            lanes = jnp.transpose(squares[t * HD:(t + 1) * HD])[:half]
            out_ref[t * per:(t + 1) * per, pl.ds(blocks * ROWS + st * half, half), :] = jnp.broadcast_to(lanes[None], (per, half, HD))


def project(x, gain, w, shards):
    blocks = w.shape[1] // HD
    return pl.pallas_call(
        project_kernel,
        out_shape=jax.ShapeDtypeStruct((shards, blocks * ROWS + 8, HD), jnp.float32),
        in_specs=[VMEM, VMEM, VMEM],
        out_specs=VMEM,
        compiler_params=params(40),
        cost_estimate=cost(2 * 512 * 512 * 1280, 6 * 2**20),
        name="project",
    )(x, gain, w)


def slot_for(ints_ref, shard, group):
    def look(j, found):
        return jnp.where(ints_ref[OWNER + shard * SLOTS + j] == group, j, found)
    return lax.fori_loop(0, SLOTS, look, 0)


def gather_kernel(low, ints_ref, pool_ref, out_ref, sems):
    me = lax.axis_index("grp")
    count = out_ref.shape[1]

    def request(j):
        return ints_ref[OWNER + me * SLOTS + j], ints_ref[LENGTH + me * SLOTS + j] - low * PAGE

    def load(j, g, p):
        return pltpu.make_async_copy(pool_ref.at[ints_ref[TABLE + j * MAXP + low + p], :, 0], out_ref.at[g, p], sems.at[j, p])

    def start(j, carry):
        g, left = request(j)
        for p in range(count):
            @pl.when(p * PAGE < left)
            def _():
                load(j, g, p).start()

            @pl.when(p * PAGE >= left)
            def _():
                out_ref[g, p] = jnp.zeros(out_ref.shape[2:], out_ref.dtype)
        return carry

    def finish(j, carry):
        g, left = request(j)
        for p in range(count):
            @pl.when(p * PAGE < left)
            def _():
                load(j, g, p).wait()

        @pl.when((left > 0) & (left < count * PAGE))
        def _():
            edge = (left - 1) // PAGE
            rows = lax.broadcasted_iota(jnp.int32, (2, PAGE, HD), 1)
            page = jnp.where(rows < left - edge * PAGE, out_ref[g, edge].astype(jnp.float32), 0.0)
            out_ref[g, edge] = page.astype(out_ref.dtype)
        return carry

    lax.fori_loop(0, SLOTS, start, 0)
    lax.fori_loop(0, SLOTS, finish, 0)


def gather_pages(low, high, ints, pool):
    shape = jax.ShapeDtypeStruct((SLOTS, high - low, 2, PAGE, HD), jnp.bfloat16)
    return pl.pallas_call(
        functools.partial(gather_kernel, low),
        out_shape=shape,
        in_specs=[SMEM, ANY],
        out_specs=VMEM,
        scratch_shapes=[pltpu.SemaphoreType.DMA((SLOTS, high - low))],
        compiler_params=params(44),
        cost_estimate=cost(0, (high - low) * 2**21),
        name="gather_pages",
    )(ints, pool)


def attend_kernel(ints_ref, *refs):
    sums_ref, pool_ref, out_ref, proj, done = refs
    me = lax.axis_index("grp")
    step = pl.program_id(0)
    block = SLOTS // pl.num_programs(0)
    scale = 1.0 / math.sqrt(HD)
    heads = out_ref.shape[2] // HD - 2
    blocks = heads + 2
    qr = STEPS * heads

    @pl.when(step == 0)
    def _():
        total = sums_ref[0]
        for i in range(1, sums_ref.shape[0]):
            total = total + sums_ref[i]
        half = 8 // STEPS
        shape = (SLOTS, HD)
        mine = lax.broadcasted_iota(jnp.int32, shape, 1) == (me % (HD // SLOTS)) * SLOTS + lax.broadcasted_iota(jnp.int32, shape, 0)
        squares = []
        for st in range(STEPS):
            row = total[blocks * ROWS + st * half:blocks * ROWS + st * half + 1]
            squares.append(jnp.sum(jnp.where(mine, jnp.broadcast_to(row, shape), 0.0), axis=-1, keepdims=True))
        inv_rms = lax.rsqrt(jnp.concatenate(squares, axis=0) / D + epsilon)
        for c in range(blocks):
            proj[c * ROWS:(c + 1) * ROWS, :] = (total[c * ROWS:(c + 1) * ROWS] * inv_rms).astype(jnp.bfloat16).astype(jnp.float32)

    lanes = lax.broadcasted_iota(jnp.int32, (qr, PAGE), 1)
    later = lax.broadcasted_iota(jnp.int32, (qr, 1), 0) % STEPS > 0
    contract = (((1,), (1,)), ((), ()))
    slots, pages, queries, scores = [], [], [], []
    for r in range(block):
        j = step * block + r
        q = proj[pl.ds(j, qr, stride=SLOTS), :]
        ids = [ints_ref[TABLE + j * MAXP + p] for p in range(MAXP)]
        slots.append(j)
        pages.append(ids)
        queries.append(q)
        scores.append([lax.dot_general(q.astype(jnp.bfloat16), pool_ref[i, 0, 0], contract, preferred_element_type=jnp.float32) * scale for i in ids])
    allowed, tops, exps, totals = [], [], [], []
    for r in range(block):
        length = ints_ref[LENGTH + me * SLOTS + slots[r]]
        allowed.append([lanes < length - p * PAGE for p in range(MAXP)])
        tops.append([jnp.max(jnp.where(ok, sc, negative_big), axis=-1, keepdims=True) for ok, sc in zip(allowed[r], scores[r])])
    for r in range(block):
        exps.append([jnp.where(ok, jnp.exp(sc - top), 0.0) for ok, sc, top in zip(allowed[r], scores[r], tops[r])])
        totals.append([jnp.sum(e, axis=-1, keepdims=True) for e in exps[r]])
    parts = []
    for r in range(block):
        parts.append([jnp.dot(e.astype(jnp.bfloat16), pool_ref[i, 1, 0], preferred_element_type=jnp.float32) for e, i in zip(exps[r], pages[r])])
    for r in range(block):
        j, q = slots[r], queries[r]
        key = [proj[pl.ds(heads * ROWS + s * SLOTS + j, 1), :] for s in range(STEPS)]
        value = [proj[pl.ds((heads + 1) * ROWS + s * SLOTS + j, 1), :] for s in range(STEPS)]
        fresh = [jnp.sum(q * k, axis=-1, keepdims=True) * scale for k in key]
        top = jnp.where(later, jnp.maximum(fresh[0], fresh[1]), fresh[0])
        e = [jnp.exp(fresh[0] - top), jnp.where(later, jnp.exp(fresh[1] - top), 0.0)]
        part = sum(w.astype(jnp.bfloat16).astype(jnp.float32) * v for w, v in zip(e, value))
        best = top
        for t in tops[r]:
            best = jnp.maximum(best, t)
        above, below = 0.0, 0.0
        for t, total, p in zip(tops[r] + [top], totals[r] + [e[0] + e[1]], parts[r] + [part]):
            factor = jnp.exp(t - best)
            above = above + p * factor
            below = below + total * factor
        done[pl.ds(j, qr, stride=SLOTS), :] = above / below

    @pl.when(step == pl.num_programs(0) - 1)
    def _():
        for c in range(blocks):
            source = done if c < heads else proj
            part = source[c * ROWS:(c + 1) * ROWS, :].astype(out_ref.dtype)
            for g in range(out_ref.shape[0]):
                out_ref[g, :, c * HD:(c + 1) * HD] = part


def attend(ints, sums, pool):
    blocks = sums.shape[1] // ROWS
    whole = lambda a: pl.BlockSpec(a.shape, lambda i, *_: (0,) * len(a.shape))
    out = jax.ShapeDtypeStruct((sums.shape[0], ROWS, blocks * HD), jnp.bfloat16)
    return pl.pallas_call(
        attend_kernel,
        out_shape=out,
        grid_spec=pltpu.PrefetchScalarGridSpec(
            num_scalar_prefetch=1,
            grid=(4,),
            in_specs=[VMEM, VMEM],
            out_specs=whole(out),
            scratch_shapes=[pltpu.VMEM((blocks * ROWS, HD), jnp.float32), pltpu.VMEM(((blocks - 2) * ROWS, HD), jnp.float32)],
        ),
        compiler_params=params(24),
        cost_estimate=cost(4 * SLOTS * MAXP * PAGE * HD * 16, 10 * 2**20),
        name="attend",
    )(ints, sums, pool)


def output_kernel(rows_ref, w_ref, *refs):
    outs, box = refs[:-1], refs[-1]
    part = lax.axis_index("tp")
    z, core = part // CORES, part % CORES
    each = rows_ref.shape[0] // box.shape[0]
    for b in range(box.shape[0]):
        lhs = rows_ref[b * each:(b + 1) * each].reshape(each * ROWS, -1)[:, :w_ref.shape[0]]
        box[b] = jnp.dot(lhs, w_ref[...], preferred_element_type=jnp.float32)
    for i, out in enumerate(outs):
        dz, dc = divmod(i, CORES)
        out[...] = box[((z + dz) % SIDE) * CORES + (core + dc) % CORES]


def output_rows(rows, w):
    parts = SIDE * CORES
    shape = jax.ShapeDtypeStruct((rows.shape[0] * ROWS // parts, w.shape[1]), jnp.float32)
    return pl.pallas_call(
        output_kernel,
        out_shape=[shape] * parts,
        in_specs=[VMEM, VMEM],
        out_specs=[VMEM] * parts,
        scratch_shapes=[pltpu.VMEM((parts,) + shape.shape, jnp.float32)],
        compiler_params=params(24),
        cost_estimate=cost(2 * 512 * 512 * 1024, 4 * 2**20),
        name="output_rows",
    )(rows, w)


def total_kernel(*refs):
    ins, out = refs[:-1], refs[-1]
    while len(ins) > 1:
        ins = [ins[i][...] + ins[i + 1][...] for i in range(0, len(ins), 2)]
    out[...] = ins[0].astype(out.dtype)


def total_rows(arrays):
    return pl.pallas_call(
        total_kernel,
        out_shape=jax.ShapeDtypeStruct(arrays[0].shape, jnp.bfloat16),
        in_specs=[VMEM] * len(arrays),
        out_specs=VMEM,
        cost_estimate=cost(0, 2**20),
        name="total_rows",
    )(*arrays)


def order_kernel(*refs):
    ins, out = refs[:-1], refs[-1]
    part = lax.axis_index("tp")
    z, core = part // CORES, part % CORES
    for i, source in enumerate(ins):
        dz, dc = divmod(i, CORES)
        block = ((z - dz + SIDE) % SIDE) * CORES + (core + dc) % CORES
        each = source.shape[0] // ROWS
        for h in range(each):
            row = pl.multiple_of((block * each + h) * SLOTS, SLOTS)
            for st in range(STEPS):
                out[st, pl.ds(row, SLOTS), :] = source[h * ROWS + st * SLOTS:h * ROWS + (st + 1) * SLOTS, :]


def order_rows(arrays):
    parts = len(arrays)
    rows, width = arrays[0].shape
    return pl.pallas_call(
        order_kernel,
        out_shape=jax.ShapeDtypeStruct((STEPS, parts * rows // STEPS, width), jnp.bfloat16),
        in_specs=[VMEM] * parts,
        out_specs=VMEM,
        cost_estimate=cost(0, 2**20),
        name="order_rows",
    )(*arrays)


def insert_kernel(low, ints_ref, rows_ref, pages_ref, *refs):
    cache_ref, box, sems = refs[-3:]
    count = pages_ref.shape[1]
    me = lax.axis_index("grp")
    first = rows_ref.shape[-1] - 2 * HD
    tile_rows = lax.broadcasted_iota(jnp.int32, (TILE, HD), 0)
    slots = lax.broadcasted_iota(jnp.int32, (SLOTS, HD), 0)
    loads = [pltpu.make_async_copy(pages_ref.at[r], box.at[r], sems.at[0, r]) for r in range(SLOTS)]
    stores = [pltpu.make_async_copy(box.at[r], cache_ref.at[r, pl.ds(low, count), :, 0], sems.at[1, r]) for r in range(SLOTS)]
    for load in loads:
        load.start()
    for r in range(SLOTS):
        slot = slot_for(ints_ref, r, me)
        at = ints_ref[LENGTH + r * SLOTS + slot]
        base = (at // TILE) * TILE

        def fill(base):
            page = base // PAGE - low

            @pl.when((page >= 0) & (page < count))
            def _():
                row = pl.multiple_of(base - (base // PAGE) * PAGE, TILE)
                for kv in range(2):
                    tile = box[r, page, kv, pl.ds(row, TILE), :].astype(jnp.float32)
                    for s in range(STEPS):
                        column = first + kv * HD
                        block = rows_ref[r, s * SLOTS:(s + 1) * SLOTS, column:column + HD].astype(jnp.float32)
                        token = jnp.sum(jnp.where(slots == slot, block, 0.0), axis=0, keepdims=True)
                        tile = jnp.where(tile_rows == at + s - base, jnp.broadcast_to(token, (TILE, HD)), tile)
                    box[r, page, kv, pl.ds(row, TILE), :] = tile.astype(box.dtype)

        loads[r].wait()
        fill(base)

        @pl.when(at - base == TILE - 1)
        def _():
            fill(base + TILE)

        stores[r].start()
    for store in stores:
        store.wait()


def insert(low, ints, rows, pages, cache):
    before = [] if cache is None else [cache]
    return pl.pallas_call(
        functools.partial(insert_kernel, low),
        out_shape=jax.ShapeDtypeStruct((SLOTS, MAXP, 2, 1, PAGE, HD), pages.dtype),
        in_specs=[SMEM, VMEM, ANY] + [ANY] * len(before),
        out_specs=ANY,
        scratch_shapes=[pltpu.VMEM(pages.shape, pages.dtype), pltpu.SemaphoreType.DMA((2, SLOTS))],
        input_output_aliases={3: 0} if before else {},
        compiler_params=params(44),
        cost_estimate=cost(0, 2 * pages.size * 2),
        name="insert_tokens",
    )(ints, rows, pages, *before)


def exchange(array):
    return lax.all_to_all(array, "grp", split_axis=0, concat_axis=0, tiled=True)


def per_device(prompt_len, request_owner, page_table, kv_pool, step_input, norm_gain, w_qkv, w_out):
    width = step_input.shape[2]
    heads = w_out.shape[1] // HD
    blocks = w_qkv.shape[2] // HD
    ints = jnp.concatenate([request_owner.reshape(-1), prompt_len, page_table.reshape(-1)])

    partial = project(step_input, norm_gain.reshape(1, width), w_qkv.reshape(width, blocks * HD), request_owner.shape[0])
    pages = [gather_pages(low, high, ints, kv_pool) for low, high in zip(CUTS, CUTS[1:])]
    mine = attend(ints, exchange(partial), kv_pool)
    rows = exchange(mine)
    received = [exchange(lax.optimization_barrier((piece, rows))[0]) for piece in pages]

    parts = output_rows(rows, w_out.reshape(heads * HD, width))
    distances = [divmod(i, CORES) for i in range(SIDE * CORES)]
    own = total_rows([parts[0]] + [move_part(parts[i], *distances[i]) for i in range(1, len(parts))])
    attn_out = order_rows([own] + [move_part(own, *d) for d in distances[1:]])

    cache = None
    for low, piece in zip(CUTS, received):
        cache = insert(low, ints, rows, piece, cache)
    return (attn_out, cache)


def solution(mesh):
    placed = (
        P(),
        P(),
        P("grp", None),
        P("grp", None, "tp", None, None),
        P(None, None, "grp"),
        P("grp"),
        P("grp", "tp", None),
        P("tp", None, "grp"),
    )
    return jax.shard_map(
        per_device,
        mesh=mesh,
        in_specs=placed,
        out_specs=(P(None, None, "grp"), P("grp", None, None, "tp", None, None)),
        check_vma=False,
    )
```

```python
import functools
import math

import jax
import jax.numpy as jnp
from jax import lax
from jax.experimental import pallas as pl
from jax.experimental.pallas import tpu as pltpu
from jax.sharding import PartitionSpec as P

D = 8192
PAGE = 128
HD = 128
MAXP = 8
STEPS = 2
TILE = 16
CORES = 2
SIDE = 4
SLOTS = 16
ROWS = STEPS * SLOTS
CUTS = (0, 4, 8)
OWNER, LENGTH, TABLE = 0, 256, 512

epsilon = 1e-05
negative_big = -1e30

HBM = pl.BlockSpec(memory_space=pltpu.HBM)
ANY = pl.BlockSpec(memory_space=pl.ANY)
SMEM = pl.BlockSpec(memory_space=pltpu.SMEM)
VMEM = pl.BlockSpec(memory_space=pltpu.VMEM)


def params(mib):
    return pltpu.CompilerParams(vmem_limit_bytes=mib * 2**20)


def cost(flops, moved):
    return pl.CostEstimate(flops=flops, bytes_accessed=moved, transcendentals=0)


def move_part(array, dz, dc):
    pairs = [(z * CORES + c, ((z + dz) % SIDE) * CORES + (c + dc) % CORES) for z in range(SIDE) for c in range(CORES)]
    return lax.ppermute(array, "tp", pairs)


def project_kernel(x_ref, gain_ref, w_ref, out_ref):
    shards = out_ref.shape[0]
    blocks = w_ref.shape[1] // HD
    gain = gain_ref[...].astype(jnp.float32)
    for st in range(STEPS):
        x = x_ref[st].astype(jnp.float32)
        squares = jnp.broadcast_to(jnp.sum(x * x, axis=-1, keepdims=True), (x.shape[0], HD))
        acc = jnp.dot((x * gain).astype(jnp.bfloat16), w_ref[...], preferred_element_type=jnp.float32)
        for c in range(blocks):
            out_ref[:, pl.ds(c * ROWS + st * SLOTS, SLOTS), :] = acc[:, c * HD:(c + 1) * HD].reshape(shards, SLOTS, HD)
        half = 8 // STEPS
        per = HD // SLOTS
        for t in range(x.shape[0] // HD):
            lanes = jnp.transpose(squares[t * HD:(t + 1) * HD])[:half]
            out_ref[t * per:(t + 1) * per, pl.ds(blocks * ROWS + st * half, half), :] = jnp.broadcast_to(lanes[None], (per, half, HD))


def project(x, gain, w, shards):
    blocks = w.shape[1] // HD
    return pl.pallas_call(
        project_kernel,
        out_shape=jax.ShapeDtypeStruct((shards, blocks * ROWS + 8, HD), jnp.float32),
        in_specs=[VMEM, VMEM, VMEM],
        out_specs=VMEM,
        compiler_params=params(40),
        cost_estimate=cost(2 * 512 * 512 * 1280, 6 * 2**20),
        name="project",
    )(x, gain, w)


def slot_for(ints_ref, shard, group):
    def look(j, found):
        return jnp.where(ints_ref[OWNER + shard * SLOTS + j] == group, j, found)
    return lax.fori_loop(0, SLOTS, look, 0)


def gather_kernel(low, ints_ref, pool_ref, out_ref, sems):
    me = lax.axis_index("grp")
    count = out_ref.shape[1]

    def request(j):
        return ints_ref[OWNER + me * SLOTS + j], ints_ref[LENGTH + me * SLOTS + j] - low * PAGE

    def load(j, g, p):
        return pltpu.make_async_copy(pool_ref.at[ints_ref[TABLE + j * MAXP + low + p], :, 0], out_ref.at[g, p], sems.at[j, p])

    def start(j, carry):
        g, left = request(j)
        for p in range(count):
            @pl.when(p * PAGE < left)
            def _():
                load(j, g, p).start()

            @pl.when(p * PAGE >= left)
            def _():
                out_ref[g, p] = jnp.zeros(out_ref.shape[2:], out_ref.dtype)
        return carry

    def finish(j, carry):
        g, left = request(j)
        for p in range(count):
            @pl.when(p * PAGE < left)
            def _():
                load(j, g, p).wait()

        @pl.when((left > 0) & (left < count * PAGE))
        def _():
            edge = (left - 1) // PAGE
            rows = lax.broadcasted_iota(jnp.int32, (2, PAGE, HD), 1)
            page = jnp.where(rows < left - edge * PAGE, out_ref[g, edge].astype(jnp.float32), 0.0)
            out_ref[g, edge] = page.astype(out_ref.dtype)
        return carry

    lax.fori_loop(0, SLOTS, start, 0)
    lax.fori_loop(0, SLOTS, finish, 0)


def gather_pages(low, high, ints, pool):
    shape = jax.ShapeDtypeStruct((SLOTS, high - low, 2, PAGE, HD), jnp.bfloat16)
    return pl.pallas_call(
        functools.partial(gather_kernel, low),
        out_shape=shape,
        in_specs=[SMEM, ANY],
        out_specs=VMEM,
        scratch_shapes=[pltpu.SemaphoreType.DMA((SLOTS, high - low))],
        compiler_params=params(44),
        cost_estimate=cost(0, (high - low) * 2**21),
        name="gather_pages",
    )(ints, pool)


def attend_kernel(ints_ref, *refs):
    sums_ref, pool_ref, out_ref, new_ref, proj, done = refs
    me = lax.axis_index("grp")
    step = pl.program_id(0)
    block = SLOTS // pl.num_programs(0)
    scale = 1.0 / math.sqrt(HD)
    heads = out_ref.shape[2] // HD - 2
    blocks = heads + 2
    qr = STEPS * heads

    @pl.when(step == 0)
    def _():
        total = sums_ref[0]
        for i in range(1, sums_ref.shape[0]):
            total = total + sums_ref[i]
        half = 8 // STEPS
        shape = (SLOTS, HD)
        mine = lax.broadcasted_iota(jnp.int32, shape, 1) == (me % (HD // SLOTS)) * SLOTS + lax.broadcasted_iota(jnp.int32, shape, 0)
        squares = []
        for st in range(STEPS):
            row = total[blocks * ROWS + st * half:blocks * ROWS + st * half + 1]
            squares.append(jnp.sum(jnp.where(mine, jnp.broadcast_to(row, shape), 0.0), axis=-1, keepdims=True))
        inv_rms = lax.rsqrt(jnp.concatenate(squares, axis=0) / D + epsilon)
        for c in range(blocks):
            proj[c * ROWS:(c + 1) * ROWS, :] = (total[c * ROWS:(c + 1) * ROWS] * inv_rms).astype(jnp.bfloat16).astype(jnp.float32)

    lanes = lax.broadcasted_iota(jnp.int32, (qr, PAGE), 1)
    later = lax.broadcasted_iota(jnp.int32, (qr, 1), 0) % STEPS > 0
    contract = (((1,), (1,)), ((), ()))
    slots, pages, queries, scores = [], [], [], []
    for r in range(block):
        j = step * block + r
        q = proj[pl.ds(j, qr, stride=SLOTS), :]
        ids = [ints_ref[TABLE + j * MAXP + p] for p in range(MAXP)]
        slots.append(j)
        pages.append(ids)
        queries.append(q)
        scores.append([lax.dot_general(q.astype(jnp.bfloat16), pool_ref[i, 0, 0], contract, preferred_element_type=jnp.float32) * scale for i in ids])
    allowed, tops, exps, totals = [], [], [], []
    for r in range(block):
        length = ints_ref[LENGTH + me * SLOTS + slots[r]]
        allowed.append([lanes < length - p * PAGE for p in range(MAXP)])
        tops.append([jnp.max(jnp.where(ok, sc, negative_big), axis=-1, keepdims=True) for ok, sc in zip(allowed[r], scores[r])])
    for r in range(block):
        exps.append([jnp.where(ok, jnp.exp(sc - top), 0.0) for ok, sc, top in zip(allowed[r], scores[r], tops[r])])
        totals.append([jnp.sum(e, axis=-1, keepdims=True) for e in exps[r]])
    parts = []
    for r in range(block):
        parts.append([jnp.dot(e.astype(jnp.bfloat16), pool_ref[i, 1, 0], preferred_element_type=jnp.float32) for e, i in zip(exps[r], pages[r])])
    for r in range(block):
        j, q = slots[r], queries[r]
        key = [proj[pl.ds(heads * ROWS + s * SLOTS + j, 1), :] for s in range(STEPS)]
        value = [proj[pl.ds((heads + 1) * ROWS + s * SLOTS + j, 1), :] for s in range(STEPS)]
        fresh = [jnp.sum(q * k, axis=-1, keepdims=True) * scale for k in key]
        top = jnp.where(later, jnp.maximum(fresh[0], fresh[1]), fresh[0])
        e = [jnp.exp(fresh[0] - top), jnp.where(later, jnp.exp(fresh[1] - top), 0.0)]
        part = sum(w.astype(jnp.bfloat16).astype(jnp.float32) * v for w, v in zip(e, value))
        best = top
        for t in tops[r]:
            best = jnp.maximum(best, t)
        above, below = 0.0, 0.0
        for t, total, p in zip(tops[r] + [top], totals[r] + [e[0] + e[1]], parts[r] + [part]):
            factor = jnp.exp(t - best)
            above = above + p * factor
            below = below + total * factor
        done[pl.ds(j, qr, stride=SLOTS), :] = above / below

    @pl.when(step == pl.num_programs(0) - 1)
    def _():
        for c in range(blocks):
            source = done if c < heads else proj
            part = source[c * ROWS:(c + 1) * ROWS, :].astype(out_ref.dtype)
            for g in range(out_ref.shape[0]):
                out_ref[g, :, c * HD:(c + 1) * HD] = part
        for kv in range(2):
            new_ref[kv] = proj[(heads + kv) * ROWS:(heads + kv + 1) * ROWS, :]


def attend(ints, sums, pool):
    blocks = sums.shape[1] // ROWS
    whole = lambda a: pl.BlockSpec(a.shape, lambda i, *_: (0,) * len(a.shape))
    out = jax.ShapeDtypeStruct((sums.shape[0], ROWS, blocks * HD), jnp.bfloat16)
    new = jax.ShapeDtypeStruct((2, ROWS, HD), jnp.float32)
    return pl.pallas_call(
        attend_kernel,
        out_shape=(out, new),
        grid_spec=pltpu.PrefetchScalarGridSpec(
            num_scalar_prefetch=1,
            grid=(4,),
            in_specs=[VMEM, VMEM],
            out_specs=(whole(out), whole(new)),
            scratch_shapes=[pltpu.VMEM((blocks * ROWS, HD), jnp.float32), pltpu.VMEM(((blocks - 2) * ROWS, HD), jnp.float32)],
        ),
        compiler_params=params(24),
        cost_estimate=cost(4 * SLOTS * MAXP * PAGE * HD * 16, 10 * 2**20),
        name="attend",
    )(ints, sums, pool)


def output_kernel(rows_ref, w_ref, *refs):
    outs, box = refs[:-1], refs[-1]
    part = lax.axis_index("tp")
    z, core = part // CORES, part % CORES
    each = rows_ref.shape[0] // box.shape[0]
    for b in range(box.shape[0]):
        lhs = rows_ref[b * each:(b + 1) * each].reshape(each * ROWS, -1)[:, :w_ref.shape[0]]
        box[b] = jnp.dot(lhs, w_ref[...], preferred_element_type=jnp.float32)
    for i, out in enumerate(outs):
        dz, dc = divmod(i, CORES)
        out[...] = box[((z + dz) % SIDE) * CORES + (core + dc) % CORES]


def output_rows(rows, w):
    parts = SIDE * CORES
    shape = jax.ShapeDtypeStruct((rows.shape[0] * ROWS // parts, w.shape[1]), jnp.float32)
    return pl.pallas_call(
        output_kernel,
        out_shape=[shape] * parts,
        in_specs=[VMEM, VMEM],
        out_specs=[VMEM] * parts,
        scratch_shapes=[pltpu.VMEM((parts,) + shape.shape, jnp.float32)],
        compiler_params=params(24),
        cost_estimate=cost(2 * 512 * 512 * 1024, 4 * 2**20),
        name="output_rows",
    )(rows, w)


def total_kernel(*refs):
    ins, out = refs[:-1], refs[-1]
    while len(ins) > 1:
        ins = [ins[i][...] + ins[i + 1][...] for i in range(0, len(ins), 2)]
    out[...] = ins[0].astype(out.dtype)


def total_rows(arrays):
    return pl.pallas_call(
        total_kernel,
        out_shape=jax.ShapeDtypeStruct(arrays[0].shape, jnp.bfloat16),
        in_specs=[VMEM] * len(arrays),
        out_specs=VMEM,
        cost_estimate=cost(0, 2**20),
        name="total_rows",
    )(*arrays)


def order_kernel(*refs):
    ins, out = refs[:-1], refs[-1]
    part = lax.axis_index("tp")
    z, core = part // CORES, part % CORES
    for i, source in enumerate(ins):
        dz, dc = divmod(i, CORES)
        block = ((z - dz + SIDE) % SIDE) * CORES + (core + dc) % CORES
        each = source.shape[0] // ROWS
        for h in range(each):
            row = pl.multiple_of((block * each + h) * SLOTS, SLOTS)
            for st in range(STEPS):
                out[st, pl.ds(row, SLOTS), :] = source[h * ROWS + st * SLOTS:h * ROWS + (st + 1) * SLOTS, :]


def order_rows(arrays):
    parts = len(arrays)
    rows, width = arrays[0].shape
    return pl.pallas_call(
        order_kernel,
        out_shape=jax.ShapeDtypeStruct((STEPS, parts * rows // STEPS, width), jnp.bfloat16),
        in_specs=[VMEM] * parts,
        out_specs=VMEM,
        cost_estimate=cost(0, 2**20),
        name="order_rows",
    )(*arrays)


def insert_kernel(low, ints_ref, rows_ref, pages_ref, *refs):
    cache_ref, box, sems = refs[-3:]
    count = pages_ref.shape[1]
    me = lax.axis_index("grp")
    first = rows_ref.shape[-1] - 2 * HD
    tile_rows = lax.broadcasted_iota(jnp.int32, (TILE, HD), 0)
    slots = lax.broadcasted_iota(jnp.int32, (SLOTS, HD), 0)
    loads = [pltpu.make_async_copy(pages_ref.at[r], box.at[r], sems.at[0, r]) for r in range(SLOTS)]
    stores = [pltpu.make_async_copy(box.at[r], cache_ref.at[r, pl.ds(low, count), :, 0], sems.at[1, r]) for r in range(SLOTS)]
    for load in loads:
        load.start()
    for r in range(SLOTS):
        slot = slot_for(ints_ref, r, me)
        at = ints_ref[LENGTH + r * SLOTS + slot]
        base = (at // TILE) * TILE

        def fill(base):
            page = base // PAGE - low

            @pl.when((page >= 0) & (page < count))
            def _():
                row = pl.multiple_of(base - (base // PAGE) * PAGE, TILE)
                for kv in range(2):
                    tile = box[r, page, kv, pl.ds(row, TILE), :].astype(jnp.float32)
                    for s in range(STEPS):
                        column = first + kv * HD
                        block = rows_ref[r, s * SLOTS:(s + 1) * SLOTS, column:column + HD].astype(jnp.float32)
                        token = jnp.sum(jnp.where(slots == slot, block, 0.0), axis=0, keepdims=True)
                        tile = jnp.where(tile_rows == at + s - base, jnp.broadcast_to(token, (TILE, HD)), tile)
                    box[r, page, kv, pl.ds(row, TILE), :] = tile.astype(box.dtype)

        loads[r].wait()
        fill(base)

        @pl.when(at - base == TILE - 1)
        def _():
            fill(base + TILE)

        stores[r].start()
    for store in stores:
        store.wait()


def insert(low, ints, rows, pages):
    return pl.pallas_call(
        functools.partial(insert_kernel, low),
        out_shape=jax.ShapeDtypeStruct((SLOTS, MAXP, 2, 1, PAGE, HD), pages.dtype),
        in_specs=[SMEM, VMEM, ANY],
        out_specs=ANY,
        scratch_shapes=[pltpu.VMEM(pages.shape, pages.dtype), pltpu.SemaphoreType.DMA((2, SLOTS))],
        compiler_params=params(44),
        cost_estimate=cost(0, 2 * pages.size * 2),
        name="insert_tokens",
    )(ints, rows, pages)


def write_kernel(low, ints_ref, new_ref, pages_in, pages_ref, box, sems):
    count = pages_ref.shape[1]
    me = lax.axis_index("grp")

    def spot(j, which):
        at = ints_ref[LENGTH + me * SLOTS + j]
        base = (at // TILE) * TILE + which * TILE
        return at, base

    def view(j, which):
        _, base = spot(j, which)
        page = base // PAGE
        row = pl.multiple_of(base - page * PAGE, TILE)
        return pages_ref.at[ints_ref[OWNER + me * SLOTS + j], page - low, :, pl.ds(row, TILE)]

    def load(j, which):
        return pltpu.make_async_copy(view(j, which), box.at[j, which], sems.at[0, j, which])

    def store(j, which):
        return pltpu.make_async_copy(box.at[j, which], view(j, which), sems.at[1, j, which])

    def each(act):
        def body(j, carry):
            at, base = spot(j, 0)

            def held(base):
                return (base >= low * PAGE) & (base < (low + count) * PAGE)

            @pl.when(held(base))
            def _():
                act(j, 0)

            @pl.when((at + STEPS > base + TILE) & held(base + TILE))
            def _():
                act(j, 1)
            return carry
        lax.fori_loop(0, SLOTS, body, 0)

    tile_rows = lax.broadcasted_iota(jnp.int32, (TILE, HD), 0)

    def fill(j, which):
        load(j, which).wait()
        at, base = spot(j, which)
        for kv in range(2):
            tile = box[j, which, kv].astype(jnp.float32)
            for s in range(STEPS):
                token = jnp.broadcast_to(new_ref[kv, pl.ds(s * SLOTS + j, 1), :], (TILE, HD))
                tile = jnp.where(tile_rows == at + s - base, token, tile)
            box[j, which, kv] = tile.astype(box.dtype)
        store(j, which).start()

    each(lambda j, which: load(j, which).start())
    each(fill)
    each(lambda j, which: store(j, which).wait())


def write_tokens(low, ints, new, pages):
    return pl.pallas_call(
        functools.partial(write_kernel, low),
        out_shape=jax.ShapeDtypeStruct(pages.shape, pages.dtype),
        in_specs=[SMEM, VMEM, ANY],
        out_specs=ANY,
        scratch_shapes=[pltpu.VMEM((SLOTS, 2, 2, TILE, HD), pages.dtype), pltpu.SemaphoreType.DMA((2, SLOTS, 2))],
        input_output_aliases={2: 0},
        compiler_params=params(54),
        cost_estimate=cost(0, 2**20),
        name="write_tokens",
    )(ints, new, pages)


def settle_kernel(low, pages_ref, cache_in, cache_ref, box, sems):
    count = pages_ref.shape[1]
    loads = [pltpu.make_async_copy(pages_ref.at[r], box.at[r], sems.at[0, r]) for r in range(SLOTS)]
    stores = [pltpu.make_async_copy(box.at[r], cache_ref.at[r, pl.ds(low, count), :, 0], sems.at[1, r]) for r in range(SLOTS)]
    for load in loads:
        load.start()
    for load, store in zip(loads, stores):
        load.wait()
        store.start()
    for store in stores:
        store.wait()


def settle(low, pages, cache):
    return pl.pallas_call(
        functools.partial(settle_kernel, low),
        out_shape=jax.ShapeDtypeStruct(cache.shape, cache.dtype),
        in_specs=[ANY, ANY],
        out_specs=ANY,
        scratch_shapes=[pltpu.VMEM(pages.shape, pages.dtype), pltpu.SemaphoreType.DMA((2, SLOTS))],
        input_output_aliases={1: 0},
        compiler_params=params(44),
        cost_estimate=cost(0, 2 * pages.size * 2),
        name="settle",
    )(pages, cache)


def exchange(array):
    return lax.all_to_all(array, "grp", split_axis=0, concat_axis=0, tiled=True)


def per_device(prompt_len, request_owner, page_table, kv_pool, step_input, norm_gain, w_qkv, w_out):
    width = step_input.shape[2]
    heads = w_out.shape[1] // HD
    blocks = w_qkv.shape[2] // HD
    ints = jnp.concatenate([request_owner.reshape(-1), prompt_len, page_table.reshape(-1)])

    partial = project(step_input, norm_gain.reshape(1, width), w_qkv.reshape(width, blocks * HD), request_owner.shape[0])
    near, far = [gather_pages(low, high, ints, kv_pool) for low, high in zip(CUTS, CUTS[1:])]
    sums = exchange(partial)
    near = exchange(lax.optimization_barrier((near, sums))[0])
    mine, new = attend(ints, sums, kv_pool)
    far = write_tokens(CUTS[1], ints, new, far)
    rows = exchange(lax.optimization_barrier((mine, near))[0])
    far = exchange(lax.optimization_barrier((far, rows))[0])

    parts = output_rows(rows, w_out.reshape(heads * HD, width))
    distances = [divmod(i, CORES) for i in range(SIDE * CORES)]
    own = total_rows([parts[0]] + [move_part(parts[i], *distances[i]) for i in range(1, len(parts))])
    attn_out = order_rows([own] + [move_part(own, *d) for d in distances[1:]])

    cache = settle(CUTS[1], far, insert(CUTS[0], ints, rows, near))
    return (attn_out, cache)


def solution(mesh):
    placed = (
        P(),
        P(),
        P("grp", None),
        P("grp", None, "tp", None, None),
        P(None, None, "grp"),
        P("grp"),
        P("grp", "tp", None),
        P("tp", None, "grp"),
    )
    return jax.shard_map(
        per_device,
        mesh=mesh,
        in_specs=placed,
        out_specs=(P(None, None, "grp"), P("grp", None, None, "tp", None, None)),
        check_vma=False,
    )
```

```python
import functools
import math

import jax
import jax.numpy as jnp
from jax import lax
from jax.experimental import pallas as pl
from jax.experimental.pallas import tpu as pltpu
from jax.sharding import PartitionSpec as P

D = 8192
PAGE = 128
HD = 128
MAXP = 8
STEPS = 2
TILE = 16
CORES = 2
SIDE = 4
SLOTS = 16
ROWS = STEPS * SLOTS
CUTS = (0, 4, 8)
OWNER, LENGTH, TABLE = 0, 256, 512

epsilon = 1e-05
negative_big = -1e30

HBM = pl.BlockSpec(memory_space=pltpu.HBM)
ANY = pl.BlockSpec(memory_space=pl.ANY)
SMEM = pl.BlockSpec(memory_space=pltpu.SMEM)
VMEM = pl.BlockSpec(memory_space=pltpu.VMEM)


def params(mib):
    return pltpu.CompilerParams(vmem_limit_bytes=mib * 2**20)


def cost(flops, moved):
    return pl.CostEstimate(flops=flops, bytes_accessed=moved, transcendentals=0)


def move(array, dy, dx):
    pairs = [(y * SIDE + x, ((y + dy) % SIDE) * SIDE + (x + dx) % SIDE) for y in range(SIDE) for x in range(SIDE)]
    return lax.ppermute(array, "grp", pairs)


def steps_back(array, dy, dx):
    line = [array]
    for _ in range(SIDE - 1):
        line.append(move(line[-1], -dy, -dx))
    return line


def move_part(array, dz, dc):
    pairs = [(z * CORES + c, ((z + dz) % SIDE) * CORES + (c + dc) % CORES) for z in range(SIDE) for c in range(CORES)]
    return lax.ppermute(array, "tp", pairs)


def project_kernel(x_ref, gain_ref, w_ref, out_ref):
    shards = out_ref.shape[0]
    blocks = w_ref.shape[1] // HD
    gain = gain_ref[...].astype(jnp.float32)
    for st in range(STEPS):
        x = x_ref[st].astype(jnp.float32)
        squares = jnp.broadcast_to(jnp.sum(x * x, axis=-1, keepdims=True), (x.shape[0], HD))
        acc = jnp.dot((x * gain).astype(jnp.bfloat16), w_ref[...], preferred_element_type=jnp.float32)
        for c in range(blocks):
            out_ref[:, pl.ds(c * ROWS + st * SLOTS, SLOTS), :] = acc[:, c * HD:(c + 1) * HD].reshape(shards, SLOTS, HD)
        half = 8 // STEPS
        per = HD // SLOTS
        for t in range(x.shape[0] // HD):
            lanes = jnp.transpose(squares[t * HD:(t + 1) * HD])[:half]
            out_ref[t * per:(t + 1) * per, pl.ds(blocks * ROWS + st * half, half), :] = jnp.broadcast_to(lanes[None], (per, half, HD))


def project(x, gain, w, shards):
    blocks = w.shape[1] // HD
    return pl.pallas_call(
        project_kernel,
        out_shape=jax.ShapeDtypeStruct((shards, blocks * ROWS + 8, HD), jnp.float32),
        in_specs=[VMEM, VMEM, VMEM],
        out_specs=VMEM,
        compiler_params=params(40),
        cost_estimate=cost(2 * 512 * 512 * 1280, 6 * 2**20),
        name="project",
    )(x, gain, w)


def slot_for(ints_ref, shard, group):
    def look(j, found):
        return jnp.where(ints_ref[OWNER + shard * SLOTS + j] == group, j, found)
    return lax.fori_loop(0, SLOTS, look, 0)


def gather_kernel(low, ints_ref, pool_ref, out_ref, sems):
    me = lax.axis_index("grp")
    count = out_ref.shape[1]

    def request(j):
        return ints_ref[OWNER + me * SLOTS + j], ints_ref[LENGTH + me * SLOTS + j] - low * PAGE

    def load(j, g, p):
        return pltpu.make_async_copy(pool_ref.at[ints_ref[TABLE + j * MAXP + low + p], :, 0], out_ref.at[g, p], sems.at[j, p])

    def start(j, carry):
        g, left = request(j)
        for p in range(count):
            @pl.when(p * PAGE < left)
            def _():
                load(j, g, p).start()

            @pl.when(p * PAGE >= left)
            def _():
                out_ref[g, p] = jnp.zeros(out_ref.shape[2:], out_ref.dtype)
        return carry

    def finish(j, carry):
        g, left = request(j)
        for p in range(count):
            @pl.when(p * PAGE < left)
            def _():
                load(j, g, p).wait()

        @pl.when((left > 0) & (left < count * PAGE))
        def _():
            edge = (left - 1) // PAGE
            rows = lax.broadcasted_iota(jnp.int32, (2, PAGE, HD), 1)
            page = jnp.where(rows < left - edge * PAGE, out_ref[g, edge].astype(jnp.float32), 0.0)
            out_ref[g, edge] = page.astype(out_ref.dtype)
        return carry

    lax.fori_loop(0, SLOTS, start, 0)
    lax.fori_loop(0, SLOTS, finish, 0)


def gather_pages(low, high, ints, pool):
    shape = jax.ShapeDtypeStruct((SLOTS, high - low, 2, PAGE, HD), jnp.bfloat16)
    return pl.pallas_call(
        functools.partial(gather_kernel, low),
        out_shape=shape,
        in_specs=[SMEM, ANY],
        out_specs=VMEM,
        scratch_shapes=[pltpu.SemaphoreType.DMA((SLOTS, high - low))],
        compiler_params=params(44),
        cost_estimate=cost(0, (high - low) * 2**21),
        name="gather_pages",
    )(ints, pool)


def attend_kernel(ints_ref, *refs):
    sums_ref, pool_ref, out_ref, new_ref, proj, done = refs
    me = lax.axis_index("grp")
    step = pl.program_id(0)
    block = SLOTS // pl.num_programs(0)
    scale = 1.0 / math.sqrt(HD)
    heads = out_ref.shape[1] // HD - 2
    blocks = heads + 2
    qr = STEPS * heads

    @pl.when(step == 0)
    def _():
        total = sums_ref[0]
        for i in range(1, sums_ref.shape[0]):
            total = total + sums_ref[i]
        half = 8 // STEPS
        shape = (SLOTS, HD)
        mine = lax.broadcasted_iota(jnp.int32, shape, 1) == (me % (HD // SLOTS)) * SLOTS + lax.broadcasted_iota(jnp.int32, shape, 0)
        squares = []
        for st in range(STEPS):
            row = total[blocks * ROWS + st * half:blocks * ROWS + st * half + 1]
            squares.append(jnp.sum(jnp.where(mine, jnp.broadcast_to(row, shape), 0.0), axis=-1, keepdims=True))
        inv_rms = lax.rsqrt(jnp.concatenate(squares, axis=0) / D + epsilon)
        for c in range(blocks):
            proj[c * ROWS:(c + 1) * ROWS, :] = (total[c * ROWS:(c + 1) * ROWS] * inv_rms).astype(jnp.bfloat16).astype(jnp.float32)

    lanes = lax.broadcasted_iota(jnp.int32, (qr, PAGE), 1)
    later = lax.broadcasted_iota(jnp.int32, (qr, 1), 0) % STEPS > 0
    contract = (((1,), (1,)), ((), ()))
    slots, pages, queries, scores = [], [], [], []
    for r in range(block):
        j = step * block + r
        q = proj[pl.ds(j, qr, stride=SLOTS), :]
        ids = [ints_ref[TABLE + j * MAXP + p] for p in range(MAXP)]
        slots.append(j)
        pages.append(ids)
        queries.append(q)
        scores.append([lax.dot_general(q.astype(jnp.bfloat16), pool_ref[i, 0, 0], contract, preferred_element_type=jnp.float32) * scale for i in ids])
    allowed, tops, exps, totals = [], [], [], []
    for r in range(block):
        length = ints_ref[LENGTH + me * SLOTS + slots[r]]
        allowed.append([lanes < length - p * PAGE for p in range(MAXP)])
        tops.append([jnp.max(jnp.where(ok, sc, negative_big), axis=-1, keepdims=True) for ok, sc in zip(allowed[r], scores[r])])
    for r in range(block):
        exps.append([jnp.where(ok, jnp.exp(sc - top), 0.0) for ok, sc, top in zip(allowed[r], scores[r], tops[r])])
        totals.append([jnp.sum(e, axis=-1, keepdims=True) for e in exps[r]])
    parts = []
    for r in range(block):
        parts.append([jnp.dot(e.astype(jnp.bfloat16), pool_ref[i, 1, 0], preferred_element_type=jnp.float32) for e, i in zip(exps[r], pages[r])])
    for r in range(block):
        j, q = slots[r], queries[r]
        key = [proj[pl.ds(heads * ROWS + s * SLOTS + j, 1), :] for s in range(STEPS)]
        value = [proj[pl.ds((heads + 1) * ROWS + s * SLOTS + j, 1), :] for s in range(STEPS)]
        fresh = [jnp.sum(q * k, axis=-1, keepdims=True) * scale for k in key]
        top = jnp.where(later, jnp.maximum(fresh[0], fresh[1]), fresh[0])
        e = [jnp.exp(fresh[0] - top), jnp.where(later, jnp.exp(fresh[1] - top), 0.0)]
        part = sum(w.astype(jnp.bfloat16).astype(jnp.float32) * v for w, v in zip(e, value))
        best = top
        for t in tops[r]:
            best = jnp.maximum(best, t)
        above, below = 0.0, 0.0
        for t, total, p in zip(tops[r] + [top], totals[r] + [e[0] + e[1]], parts[r] + [part]):
            factor = jnp.exp(t - best)
            above = above + p * factor
            below = below + total * factor
        done[pl.ds(j, qr, stride=SLOTS), :] = above / below

    @pl.when(step == pl.num_programs(0) - 1)
    def _():
        for c in range(blocks):
            source = done if c < heads else proj
            out_ref[:, c * HD:(c + 1) * HD] = source[c * ROWS:(c + 1) * ROWS, :].astype(out_ref.dtype)
        for kv in range(2):
            new_ref[kv] = proj[(heads + kv) * ROWS:(heads + kv + 1) * ROWS, :]


def attend(ints, sums, pool):
    blocks = sums.shape[1] // ROWS
    whole = lambda a: pl.BlockSpec(a.shape, lambda i, *_: (0,) * len(a.shape))
    out = jax.ShapeDtypeStruct((ROWS, blocks * HD), jnp.bfloat16)
    new = jax.ShapeDtypeStruct((2, ROWS, HD), jnp.float32)
    return pl.pallas_call(
        attend_kernel,
        out_shape=(out, new),
        grid_spec=pltpu.PrefetchScalarGridSpec(
            num_scalar_prefetch=1,
            grid=(4,),
            in_specs=[VMEM, VMEM],
            out_specs=(whole(out), whole(new)),
            scratch_shapes=[pltpu.VMEM((blocks * ROWS, HD), jnp.float32), pltpu.VMEM(((blocks - 2) * ROWS, HD), jnp.float32)],
        ),
        compiler_params=params(24),
        cost_estimate=cost(4 * SLOTS * MAXP * PAGE * HD * 16, 10 * 2**20),
        name="attend",
    )(ints, sums, pool)


def arrange_kernel(*refs):
    ins, out = refs[:-1], refs[-1]
    me = lax.axis_index("grp")
    y, x = me // SIDE, me % SIDE
    pieces = len(ins) // SIDE
    for i, piece in enumerate(ins):
        part, ix = divmod(i, SIDE)
        each = SIDE // pieces
        for k in range(each):
            iy = part * each + k
            out[((y + iy) % SIDE) * SIDE + (x + ix) % SIDE] = piece[k]


def arrange(arrays):
    shape = (SIDE * SIDE,) + arrays[0].shape[1:]
    return pl.pallas_call(
        arrange_kernel,
        out_shape=jax.ShapeDtypeStruct(shape, arrays[0].dtype),
        in_specs=[VMEM] * len(arrays),
        out_specs=VMEM,
        compiler_params=params(20),
        cost_estimate=cost(0, 3 * 2**20),
        name="arrange",
    )(*arrays)


def output_kernel(rows_ref, w_ref, *refs):
    outs, box = refs[:-1], refs[-1]
    part = lax.axis_index("tp")
    z, core = part // CORES, part % CORES
    each = rows_ref.shape[0] // box.shape[0]
    for b in range(box.shape[0]):
        lhs = rows_ref[b * each:(b + 1) * each].reshape(each * ROWS, -1)[:, :w_ref.shape[0]]
        box[b] = jnp.dot(lhs, w_ref[...], preferred_element_type=jnp.float32)
    for i, out in enumerate(outs):
        dz, dc = divmod(i, CORES)
        out[...] = box[((z + dz) % SIDE) * CORES + (core + dc) % CORES]


def output_rows(rows, w):
    parts = SIDE * CORES
    shape = jax.ShapeDtypeStruct((rows.shape[0] * ROWS // parts, w.shape[1]), jnp.float32)
    return pl.pallas_call(
        output_kernel,
        out_shape=[shape] * parts,
        in_specs=[VMEM, VMEM],
        out_specs=[VMEM] * parts,
        scratch_shapes=[pltpu.VMEM((parts,) + shape.shape, jnp.float32)],
        compiler_params=params(24),
        cost_estimate=cost(2 * 512 * 512 * 1024, 4 * 2**20),
        name="output_rows",
    )(rows, w)


def total_kernel(*refs):
    ins, out = refs[:-1], refs[-1]
    while len(ins) > 1:
        ins = [ins[i][...] + ins[i + 1][...] for i in range(0, len(ins), 2)]
    out[...] = ins[0].astype(out.dtype)


def total_rows(arrays):
    return pl.pallas_call(
        total_kernel,
        out_shape=jax.ShapeDtypeStruct(arrays[0].shape, jnp.bfloat16),
        in_specs=[VMEM] * len(arrays),
        out_specs=VMEM,
        cost_estimate=cost(0, 2**20),
        name="total_rows",
    )(*arrays)


def order_kernel(*refs):
    ins, out = refs[:-1], refs[-1]
    part = lax.axis_index("tp")
    z, core = part // CORES, part % CORES
    for i, source in enumerate(ins):
        dz, dc = divmod(i, CORES)
        block = ((z - dz + SIDE) % SIDE) * CORES + (core + dc) % CORES
        each = source.shape[0] // ROWS
        for h in range(each):
            row = pl.multiple_of((block * each + h) * SLOTS, SLOTS)
            for st in range(STEPS):
                out[st, pl.ds(row, SLOTS), :] = source[h * ROWS + st * SLOTS:h * ROWS + (st + 1) * SLOTS, :]


def order_rows(arrays):
    parts = len(arrays)
    rows, width = arrays[0].shape
    return pl.pallas_call(
        order_kernel,
        out_shape=jax.ShapeDtypeStruct((STEPS, parts * rows // STEPS, width), jnp.bfloat16),
        in_specs=[VMEM] * parts,
        out_specs=VMEM,
        cost_estimate=cost(0, 2**20),
        name="order_rows",
    )(*arrays)


def insert_kernel(low, ints_ref, rows_ref, pages_ref, *refs):
    cache_ref, box, sems = refs[-3:]
    count = pages_ref.shape[1]
    me = lax.axis_index("grp")
    first = rows_ref.shape[-1] - 2 * HD
    tile_rows = lax.broadcasted_iota(jnp.int32, (TILE, HD), 0)
    slots = lax.broadcasted_iota(jnp.int32, (SLOTS, HD), 0)
    loads = [pltpu.make_async_copy(pages_ref.at[r], box.at[r], sems.at[0, r]) for r in range(SLOTS)]
    stores = [pltpu.make_async_copy(box.at[r], cache_ref.at[r, pl.ds(low, count), :, 0], sems.at[1, r]) for r in range(SLOTS)]
    for load in loads:
        load.start()
    for r in range(SLOTS):
        slot = slot_for(ints_ref, r, me)
        at = ints_ref[LENGTH + r * SLOTS + slot]
        base = (at // TILE) * TILE

        def fill(base):
            page = base // PAGE - low

            @pl.when((page >= 0) & (page < count))
            def _():
                row = pl.multiple_of(base - (base // PAGE) * PAGE, TILE)
                for kv in range(2):
                    tile = box[r, page, kv, pl.ds(row, TILE), :].astype(jnp.float32)
                    for s in range(STEPS):
                        column = first + kv * HD
                        block = rows_ref[r, s * SLOTS:(s + 1) * SLOTS, column:column + HD].astype(jnp.float32)
                        token = jnp.sum(jnp.where(slots == slot, block, 0.0), axis=0, keepdims=True)
                        tile = jnp.where(tile_rows == at + s - base, jnp.broadcast_to(token, (TILE, HD)), tile)
                    box[r, page, kv, pl.ds(row, TILE), :] = tile.astype(box.dtype)

        loads[r].wait()
        fill(base)

        @pl.when(at - base == TILE - 1)
        def _():
            fill(base + TILE)

        stores[r].start()
    for store in stores:
        store.wait()


def insert(low, ints, rows, pages):
    return pl.pallas_call(
        functools.partial(insert_kernel, low),
        out_shape=jax.ShapeDtypeStruct((SLOTS, MAXP, 2, 1, PAGE, HD), pages.dtype),
        in_specs=[SMEM, VMEM, ANY],
        out_specs=ANY,
        scratch_shapes=[pltpu.VMEM(pages.shape, pages.dtype), pltpu.SemaphoreType.DMA((2, SLOTS))],
        compiler_params=params(44),
        cost_estimate=cost(0, 2 * pages.size * 2),
        name="insert_tokens",
    )(ints, rows, pages)


def write_kernel(low, ints_ref, new_ref, pages_in, pages_ref, box, sems):
    count = pages_ref.shape[1]
    me = lax.axis_index("grp")

    def spot(j, which):
        at = ints_ref[LENGTH + me * SLOTS + j]
        base = (at // TILE) * TILE + which * TILE
        return at, base

    def view(j, which):
        _, base = spot(j, which)
        page = base // PAGE
        row = pl.multiple_of(base - page * PAGE, TILE)
        return pages_ref.at[ints_ref[OWNER + me * SLOTS + j], page - low, :, pl.ds(row, TILE)]

    def load(j, which):
        return pltpu.make_async_copy(view(j, which), box.at[j, which], sems.at[0, j, which])

    def store(j, which):
        return pltpu.make_async_copy(box.at[j, which], view(j, which), sems.at[1, j, which])

    def each(act):
        def body(j, carry):
            at, base = spot(j, 0)

            def held(base):
                return (base >= low * PAGE) & (base < (low + count) * PAGE)

            @pl.when(held(base))
            def _():
                act(j, 0)

            @pl.when((at + STEPS > base + TILE) & held(base + TILE))
            def _():
                act(j, 1)
            return carry
        lax.fori_loop(0, SLOTS, body, 0)

    tile_rows = lax.broadcasted_iota(jnp.int32, (TILE, HD), 0)

    def fill(j, which):
        load(j, which).wait()
        at, base = spot(j, which)
        for kv in range(2):
            tile = box[j, which, kv].astype(jnp.float32)
            for s in range(STEPS):
                token = jnp.broadcast_to(new_ref[kv, pl.ds(s * SLOTS + j, 1), :], (TILE, HD))
                tile = jnp.where(tile_rows == at + s - base, token, tile)
            box[j, which, kv] = tile.astype(box.dtype)
        store(j, which).start()

    each(lambda j, which: load(j, which).start())
    each(fill)
    each(lambda j, which: store(j, which).wait())


def write_tokens(low, ints, new, pages):
    return pl.pallas_call(
        functools.partial(write_kernel, low),
        out_shape=jax.ShapeDtypeStruct(pages.shape, pages.dtype),
        in_specs=[SMEM, VMEM, ANY],
        out_specs=ANY,
        scratch_shapes=[pltpu.VMEM((SLOTS, 2, 2, TILE, HD), pages.dtype), pltpu.SemaphoreType.DMA((2, SLOTS, 2))],
        input_output_aliases={2: 0},
        compiler_params=params(54),
        cost_estimate=cost(0, 2**20),
        name="write_tokens",
    )(ints, new, pages)


def settle_kernel(low, pages_ref, cache_in, cache_ref, box, sems):
    count = pages_ref.shape[1]
    loads = [pltpu.make_async_copy(pages_ref.at[r], box.at[r], sems.at[0, r]) for r in range(SLOTS)]
    stores = [pltpu.make_async_copy(box.at[r], cache_ref.at[r, pl.ds(low, count), :, 0], sems.at[1, r]) for r in range(SLOTS)]
    for load in loads:
        load.start()
    for load, store in zip(loads, stores):
        load.wait()
        store.start()
    for store in stores:
        store.wait()


def settle(low, pages, cache):
    return pl.pallas_call(
        functools.partial(settle_kernel, low),
        out_shape=jax.ShapeDtypeStruct(cache.shape, cache.dtype),
        in_specs=[ANY, ANY],
        out_specs=ANY,
        scratch_shapes=[pltpu.VMEM(pages.shape, pages.dtype), pltpu.SemaphoreType.DMA((2, SLOTS))],
        input_output_aliases={1: 0},
        compiler_params=params(44),
        cost_estimate=cost(0, 2 * pages.size * 2),
        name="settle",
    )(pages, cache)


def exchange(array):
    return lax.all_to_all(array, "grp", split_axis=0, concat_axis=0, tiled=True)


def per_device(prompt_len, request_owner, page_table, kv_pool, step_input, norm_gain, w_qkv, w_out):
    width = step_input.shape[2]
    heads = w_out.shape[1] // HD
    blocks = w_qkv.shape[2] // HD
    ints = jnp.concatenate([request_owner.reshape(-1), prompt_len, page_table.reshape(-1)])

    partial = project(step_input, norm_gain.reshape(1, width), w_qkv.reshape(width, blocks * HD), request_owner.shape[0])
    near, far = [gather_pages(low, high, ints, kv_pool) for low, high in zip(CUTS, CUTS[1:])]
    sums = exchange(partial)
    near = exchange(lax.optimization_barrier((near, sums))[0])
    mine, new = attend(ints, sums, kv_pool)
    far = write_tokens(CUTS[1], ints, new, far)
    line = steps_back(mine, 1, 0)
    pieces = steps_back(jnp.stack(line[:2]), 0, 1) + steps_back(jnp.stack(line[2:]), 0, 1)
    far = exchange(lax.optimization_barrier((far, pieces))[0])
    rows = arrange(pieces)

    parts = output_rows(rows, w_out.reshape(heads * HD, width))
    distances = [divmod(i, CORES) for i in range(SIDE * CORES)]
    own = total_rows([parts[0]] + [move_part(parts[i], *distances[i]) for i in range(1, len(parts))])
    attn_out = order_rows([own] + [move_part(own, *d) for d in distances[1:]])

    cache = settle(CUTS[1], far, insert(CUTS[0], ints, rows, near))
    return (attn_out, cache)


def solution(mesh):
    placed = (
        P(),
        P(),
        P("grp", None),
        P("grp", None, "tp", None, None),
        P(None, None, "grp"),
        P("grp"),
        P("grp", "tp", None),
        P("tp", None, "grp"),
    )
    return jax.shard_map(
        per_device,
        mesh=mesh,
        in_specs=placed,
        out_specs=(P(None, None, "grp"), P("grp", None, None, "tp", None, None)),
        check_vma=False,
    )
```

```python
import functools
import math

import jax
import jax.numpy as jnp
from jax import lax
from jax.experimental import pallas as pl
from jax.experimental.pallas import tpu as pltpu
from jax.sharding import PartitionSpec as P

D = 8192
PAGE = 128
HD = 128
MAXP = 8
STEPS = 2
TILE = 16
CORES = 2
SIDE = 4
SLOTS = 16
ROWS = STEPS * SLOTS
CUTS = (0, 4, 8)
OWNER, LENGTH, TABLE = 0, 256, 512

epsilon = 1e-05
negative_big = -1e30

HBM = pl.BlockSpec(memory_space=pltpu.HBM)
ANY = pl.BlockSpec(memory_space=pl.ANY)
SMEM = pl.BlockSpec(memory_space=pltpu.SMEM)
VMEM = pl.BlockSpec(memory_space=pltpu.VMEM)


def params(mib):
    return pltpu.CompilerParams(vmem_limit_bytes=mib * 2**20)


def cost(flops, moved):
    return pl.CostEstimate(flops=flops, bytes_accessed=moved, transcendentals=0)


def move(array, dy, dx):
    pairs = [(y * SIDE + x, ((y + dy) % SIDE) * SIDE + (x + dx) % SIDE) for y in range(SIDE) for x in range(SIDE)]
    return lax.ppermute(array, "grp", pairs)


def steps_back(array, dy, dx):
    line = [array]
    for _ in range(SIDE - 1):
        line.append(move(line[-1], -dy, -dx))
    return line


def move_part(array, dz, dc):
    pairs = [(z * CORES + c, ((z + dz) % SIDE) * CORES + (c + dc) % CORES) for z in range(SIDE) for c in range(CORES)]
    return lax.ppermute(array, "tp", pairs)


def project_kernel(x_ref, gain_ref, w_ref, out_ref):
    shards = out_ref.shape[0]
    blocks = w_ref.shape[1] // HD
    gain = gain_ref[...].astype(jnp.float32)
    for st in range(STEPS):
        x = x_ref[st].astype(jnp.float32)
        squares = jnp.broadcast_to(jnp.sum(x * x, axis=-1, keepdims=True), (x.shape[0], HD))
        acc = jnp.dot((x * gain).astype(jnp.bfloat16), w_ref[...], preferred_element_type=jnp.float32)
        for c in range(blocks):
            out_ref[:, pl.ds(c * ROWS + st * SLOTS, SLOTS), :] = acc[:, c * HD:(c + 1) * HD].reshape(shards, SLOTS, HD)
        half = 8 // STEPS
        per = HD // SLOTS
        for t in range(x.shape[0] // HD):
            lanes = jnp.transpose(squares[t * HD:(t + 1) * HD])[:half]
            out_ref[t * per:(t + 1) * per, pl.ds(blocks * ROWS + st * half, half), :] = jnp.broadcast_to(lanes[None], (per, half, HD))


def project(x, gain, w, shards):
    blocks = w.shape[1] // HD
    return pl.pallas_call(
        project_kernel,
        out_shape=jax.ShapeDtypeStruct((shards, blocks * ROWS + 8, HD), jnp.float32),
        in_specs=[VMEM, VMEM, VMEM],
        out_specs=VMEM,
        compiler_params=params(40),
        cost_estimate=cost(2 * 512 * 512 * 1280, 6 * 2**20),
        name="project",
    )(x, gain, w)


def slot_for(ints_ref, shard, group):
    def look(j, found):
        return jnp.where(ints_ref[OWNER + shard * SLOTS + j] == group, j, found)
    return lax.fori_loop(0, SLOTS, look, 0)


def gather_kernel(low, ints_ref, pool_ref, out_ref, sems):
    me = lax.axis_index("grp")
    count = out_ref.shape[1]

    def request(j):
        return ints_ref[OWNER + me * SLOTS + j], ints_ref[LENGTH + me * SLOTS + j] - low * PAGE

    def load(j, g, p):
        return pltpu.make_async_copy(pool_ref.at[ints_ref[TABLE + j * MAXP + low + p], :, 0], out_ref.at[g, p], sems.at[j, p])

    def start(j, carry):
        g, left = request(j)
        for p in range(count):
            @pl.when(p * PAGE < left)
            def _():
                load(j, g, p).start()

            @pl.when(p * PAGE >= left)
            def _():
                out_ref[g, p] = jnp.zeros(out_ref.shape[2:], out_ref.dtype)
        return carry

    def finish(j, carry):
        g, left = request(j)
        for p in range(count):
            @pl.when(p * PAGE < left)
            def _():
                load(j, g, p).wait()

        @pl.when((left > 0) & (left < count * PAGE))
        def _():
            edge = (left - 1) // PAGE
            rows = lax.broadcasted_iota(jnp.int32, (2, PAGE, HD), 1)
            page = jnp.where(rows < left - edge * PAGE, out_ref[g, edge].astype(jnp.float32), 0.0)
            out_ref[g, edge] = page.astype(out_ref.dtype)
        return carry

    lax.fori_loop(0, SLOTS, start, 0)
    lax.fori_loop(0, SLOTS, finish, 0)


def gather_pages(low, high, ints, pool):
    shape = jax.ShapeDtypeStruct((SLOTS, high - low, 2, PAGE, HD), jnp.bfloat16)
    return pl.pallas_call(
        functools.partial(gather_kernel, low),
        out_shape=shape,
        in_specs=[SMEM, ANY],
        out_specs=VMEM,
        scratch_shapes=[pltpu.SemaphoreType.DMA((SLOTS, high - low))],
        compiler_params=params(44),
        cost_estimate=cost(0, (high - low) * 2**21),
        name="gather_pages",
    )(ints, pool)


def attend_kernel(ints_ref, *refs):
    sums_ref, pool_ref, out_ref, new_ref, proj, done = refs
    me = lax.axis_index("grp")
    step = pl.program_id(0)
    block = SLOTS // pl.num_programs(0)
    scale = 1.0 / math.sqrt(HD)
    heads = out_ref.shape[1] // HD - 2
    blocks = heads + 2
    qr = STEPS * heads

    @pl.when(step == 0)
    def _():
        total = sums_ref[0]
        for i in range(1, sums_ref.shape[0]):
            total = total + sums_ref[i]
        half = 8 // STEPS
        shape = (SLOTS, HD)
        mine = lax.broadcasted_iota(jnp.int32, shape, 1) == (me % (HD // SLOTS)) * SLOTS + lax.broadcasted_iota(jnp.int32, shape, 0)
        squares = []
        for st in range(STEPS):
            row = total[blocks * ROWS + st * half:blocks * ROWS + st * half + 1]
            squares.append(jnp.sum(jnp.where(mine, jnp.broadcast_to(row, shape), 0.0), axis=-1, keepdims=True))
        inv_rms = lax.rsqrt(jnp.concatenate(squares, axis=0) / D + epsilon)
        for c in range(blocks):
            proj[c * ROWS:(c + 1) * ROWS, :] = (total[c * ROWS:(c + 1) * ROWS] * inv_rms).astype(jnp.bfloat16).astype(jnp.float32)

    lanes = lax.broadcasted_iota(jnp.int32, (qr, PAGE), 1)
    later = lax.broadcasted_iota(jnp.int32, (qr, 1), 0) % STEPS > 0
    contract = (((1,), (1,)), ((), ()))
    slots, pages, queries, scores = [], [], [], []
    for r in range(block):
        j = step * block + r
        q = proj[pl.ds(j, qr, stride=SLOTS), :]
        ids = [ints_ref[TABLE + j * MAXP + p] for p in range(MAXP)]
        slots.append(j)
        pages.append(ids)
        queries.append(q)
        scores.append([lax.dot_general(q.astype(jnp.bfloat16), pool_ref[i, 0, 0], contract, preferred_element_type=jnp.float32) * scale for i in ids])
    allowed, tops, exps, totals = [], [], [], []
    for r in range(block):
        length = ints_ref[LENGTH + me * SLOTS + slots[r]]
        allowed.append([lanes < length - p * PAGE for p in range(MAXP)])
        tops.append([jnp.max(jnp.where(ok, sc, negative_big), axis=-1, keepdims=True) for ok, sc in zip(allowed[r], scores[r])])
    for r in range(block):
        exps.append([jnp.where(ok, jnp.exp(sc - top), 0.0) for ok, sc, top in zip(allowed[r], scores[r], tops[r])])
        totals.append([jnp.sum(e, axis=-1, keepdims=True) for e in exps[r]])
    parts = []
    for r in range(block):
        parts.append([jnp.dot(e.astype(jnp.bfloat16), pool_ref[i, 1, 0], preferred_element_type=jnp.float32) for e, i in zip(exps[r], pages[r])])
    for r in range(block):
        j, q = slots[r], queries[r]
        key = [proj[pl.ds(heads * ROWS + s * SLOTS + j, 1), :] for s in range(STEPS)]
        value = [proj[pl.ds((heads + 1) * ROWS + s * SLOTS + j, 1), :] for s in range(STEPS)]
        fresh = [jnp.sum(q * k, axis=-1, keepdims=True) * scale for k in key]
        top = jnp.where(later, jnp.maximum(fresh[0], fresh[1]), fresh[0])
        e = [jnp.exp(fresh[0] - top), jnp.where(later, jnp.exp(fresh[1] - top), 0.0)]
        part = sum(w.astype(jnp.bfloat16).astype(jnp.float32) * v for w, v in zip(e, value))
        best = top
        for t in tops[r]:
            best = jnp.maximum(best, t)
        above, below = 0.0, 0.0
        for t, total, p in zip(tops[r] + [top], totals[r] + [e[0] + e[1]], parts[r] + [part]):
            factor = jnp.exp(t - best)
            above = above + p * factor
            below = below + total * factor
        done[pl.ds(j, qr, stride=SLOTS), :] = above / below

    @pl.when(step == pl.num_programs(0) - 1)
    def _():
        for c in range(blocks):
            source = done if c < heads else proj
            out_ref[:, c * HD:(c + 1) * HD] = source[c * ROWS:(c + 1) * ROWS, :].astype(out_ref.dtype)
        for kv in range(2):
            new_ref[kv] = proj[(heads + kv) * ROWS:(heads + kv + 1) * ROWS, :]


def attend(ints, sums, pool):
    blocks = sums.shape[1] // ROWS
    whole = lambda a: pl.BlockSpec(a.shape, lambda i, *_: (0,) * len(a.shape))
    out = jax.ShapeDtypeStruct((ROWS, blocks * HD), jnp.bfloat16)
    new = jax.ShapeDtypeStruct((2, ROWS, HD), jnp.float32)
    return pl.pallas_call(
        attend_kernel,
        out_shape=(out, new),
        grid_spec=pltpu.PrefetchScalarGridSpec(
            num_scalar_prefetch=1,
            grid=(4,),
            in_specs=[VMEM, VMEM],
            out_specs=(whole(out), whole(new)),
            scratch_shapes=[pltpu.VMEM((blocks * ROWS, HD), jnp.float32), pltpu.VMEM(((blocks - 2) * ROWS, HD), jnp.float32)],
        ),
        compiler_params=params(24),
        cost_estimate=cost(4 * SLOTS * MAXP * PAGE * HD * 16, 10 * 2**20),
        name="attend",
    )(ints, sums, pool)


def arrange_kernel(*refs):
    ins, out = refs[:-1], refs[-1]
    me = lax.axis_index("grp")
    y, x = me // SIDE, me % SIDE
    pieces = len(ins) // SIDE
    for i, piece in enumerate(ins):
        part, ix = divmod(i, SIDE)
        each = SIDE // pieces
        for k in range(each):
            iy = part * each + k
            out[((y + iy) % SIDE) * SIDE + (x + ix) % SIDE] = piece[k]


def arrange(arrays):
    shape = (SIDE * SIDE,) + arrays[0].shape[1:]
    return pl.pallas_call(
        arrange_kernel,
        out_shape=jax.ShapeDtypeStruct(shape, arrays[0].dtype),
        in_specs=[VMEM] * len(arrays),
        out_specs=VMEM,
        compiler_params=params(20),
        cost_estimate=cost(0, 3 * 2**20),
        name="arrange",
    )(*arrays)


def output_kernel(rows_ref, w_ref, *refs):
    outs, box = refs[:-1], refs[-1]
    part = lax.axis_index("tp")
    z, core = part // CORES, part % CORES
    each = rows_ref.shape[0] // box.shape[0]
    for b in range(box.shape[0]):
        lhs = rows_ref[b * each:(b + 1) * each].reshape(each * ROWS, -1)[:, :w_ref.shape[0]]
        box[b] = jnp.dot(lhs, w_ref[...], preferred_element_type=jnp.float32)
    for i, out in enumerate(outs):
        dz, dc = divmod(i, CORES)
        out[...] = box[((z + dz) % SIDE) * CORES + (core + dc) % CORES]


def output_rows(rows, w):
    parts = SIDE * CORES
    shape = jax.ShapeDtypeStruct((rows.shape[0] * ROWS // parts, w.shape[1]), jnp.float32)
    return pl.pallas_call(
        output_kernel,
        out_shape=[shape] * parts,
        in_specs=[VMEM, VMEM],
        out_specs=[VMEM] * parts,
        scratch_shapes=[pltpu.VMEM((parts,) + shape.shape, jnp.float32)],
        compiler_params=params(24),
        cost_estimate=cost(2 * 512 * 512 * 1024, 4 * 2**20),
        name="output_rows",
    )(rows, w)


def total_kernel(*refs):
    ins, out = refs[:-1], refs[-1]
    while len(ins) > 1:
        ins = [ins[i][...] + ins[i + 1][...] for i in range(0, len(ins), 2)]
    out[...] = ins[0].astype(out.dtype)


def total_rows(arrays):
    return pl.pallas_call(
        total_kernel,
        out_shape=jax.ShapeDtypeStruct(arrays[0].shape, jnp.bfloat16),
        in_specs=[VMEM] * len(arrays),
        out_specs=VMEM,
        cost_estimate=cost(0, 2**20),
        name="total_rows",
    )(*arrays)


def order_kernel(*refs):
    ins, out = refs[:-1], refs[-1]
    part = lax.axis_index("tp")
    z, core = part // CORES, part % CORES
    for i, source in enumerate(ins):
        dz, dc = divmod(i, CORES)
        block = ((z - dz + SIDE) % SIDE) * CORES + (core + dc) % CORES
        each = source.shape[0] // ROWS
        for h in range(each):
            row = pl.multiple_of((block * each + h) * SLOTS, SLOTS)
            for st in range(STEPS):
                out[st, pl.ds(row, SLOTS), :] = source[h * ROWS + st * SLOTS:h * ROWS + (st + 1) * SLOTS, :]


def order_rows(arrays):
    parts = len(arrays)
    rows, width = arrays[0].shape
    return pl.pallas_call(
        order_kernel,
        out_shape=jax.ShapeDtypeStruct((STEPS, parts * rows // STEPS, width), jnp.bfloat16),
        in_specs=[VMEM] * parts,
        out_specs=VMEM,
        cost_estimate=cost(0, 2**20),
        name="order_rows",
    )(*arrays)


def insert_kernel(low, ints_ref, rows_ref, pages_ref, *refs):
    cache_ref, box, sems = refs[-3:]
    count = pages_ref.shape[1]
    me = lax.axis_index("grp")
    first = rows_ref.shape[-1] - 2 * HD
    tile_rows = lax.broadcasted_iota(jnp.int32, (TILE, HD), 0)
    slots = lax.broadcasted_iota(jnp.int32, (SLOTS, HD), 0)
    loads = [pltpu.make_async_copy(pages_ref.at[r], box.at[r], sems.at[0, r]) for r in range(SLOTS)]
    stores = [pltpu.make_async_copy(box.at[r], cache_ref.at[r, pl.ds(low, count), :, 0], sems.at[1, r]) for r in range(SLOTS)]
    for load in loads:
        load.start()
    for r in range(SLOTS):
        slot = slot_for(ints_ref, r, me)
        at = ints_ref[LENGTH + r * SLOTS + slot]
        base = (at // TILE) * TILE

        def fill(base):
            page = base // PAGE - low

            @pl.when((page >= 0) & (page < count))
            def _():
                row = pl.multiple_of(base - (base // PAGE) * PAGE, TILE)
                for kv in range(2):
                    tile = box[r, page, kv, pl.ds(row, TILE), :].astype(jnp.float32)
                    for s in range(STEPS):
                        column = first + kv * HD
                        block = rows_ref[r, s * SLOTS:(s + 1) * SLOTS, column:column + HD].astype(jnp.float32)
                        token = jnp.sum(jnp.where(slots == slot, block, 0.0), axis=0, keepdims=True)
                        tile = jnp.where(tile_rows == at + s - base, jnp.broadcast_to(token, (TILE, HD)), tile)
                    box[r, page, kv, pl.ds(row, TILE), :] = tile.astype(box.dtype)

        loads[r].wait()
        fill(base)

        @pl.when(at - base == TILE - 1)
        def _():
            fill(base + TILE)

        stores[r].start()
    for store in stores:
        store.wait()


def insert(low, ints, rows, pages):
    return pl.pallas_call(
        functools.partial(insert_kernel, low),
        out_shape=jax.ShapeDtypeStruct((SLOTS, MAXP, 2, 1, PAGE, HD), pages.dtype),
        in_specs=[SMEM, VMEM, ANY],
        out_specs=ANY,
        scratch_shapes=[pltpu.VMEM(pages.shape, pages.dtype), pltpu.SemaphoreType.DMA((2, SLOTS))],
        compiler_params=params(44),
        cost_estimate=cost(0, 2 * pages.size * 2),
        name="insert_tokens",
    )(ints, rows, pages)


def write_kernel(low, ints_ref, new_ref, pages_in, pages_ref, box, sems):
    count = pages_ref.shape[1]
    me = lax.axis_index("grp")

    def spot(j, which):
        at = ints_ref[LENGTH + me * SLOTS + j]
        base = (at // TILE) * TILE + which * TILE
        return at, base

    def view(j, which):
        _, base = spot(j, which)
        page = base // PAGE
        row = pl.multiple_of(base - page * PAGE, TILE)
        return pages_ref.at[ints_ref[OWNER + me * SLOTS + j], page - low, :, pl.ds(row, TILE)]

    def load(j, which):
        return pltpu.make_async_copy(view(j, which), box.at[j, which], sems.at[0, j, which])

    def store(j, which):
        return pltpu.make_async_copy(box.at[j, which], view(j, which), sems.at[1, j, which])

    def each(act):
        def body(j, carry):
            at, base = spot(j, 0)

            def held(base):
                return (base >= low * PAGE) & (base < (low + count) * PAGE)

            @pl.when(held(base))
            def _():
                act(j, 0)

            @pl.when((at + STEPS > base + TILE) & held(base + TILE))
            def _():
                act(j, 1)
            return carry
        lax.fori_loop(0, SLOTS, body, 0)

    tile_rows = lax.broadcasted_iota(jnp.int32, (TILE, HD), 0)

    def fill(j, which):
        load(j, which).wait()
        at, base = spot(j, which)
        for kv in range(2):
            tile = box[j, which, kv].astype(jnp.float32)
            for s in range(STEPS):
                token = jnp.broadcast_to(new_ref[kv, pl.ds(s * SLOTS + j, 1), :], (TILE, HD))
                tile = jnp.where(tile_rows == at + s - base, token, tile)
            box[j, which, kv] = tile.astype(box.dtype)
        store(j, which).start()

    each(lambda j, which: load(j, which).start())
    each(fill)
    each(lambda j, which: store(j, which).wait())


def write_tokens(low, ints, new, pages):
    return pl.pallas_call(
        functools.partial(write_kernel, low),
        out_shape=jax.ShapeDtypeStruct(pages.shape, pages.dtype),
        in_specs=[SMEM, VMEM, ANY],
        out_specs=ANY,
        scratch_shapes=[pltpu.VMEM((SLOTS, 2, 2, TILE, HD), pages.dtype), pltpu.SemaphoreType.DMA((2, SLOTS, 2))],
        input_output_aliases={2: 0},
        compiler_params=params(54),
        cost_estimate=cost(0, 2**20),
        name="write_tokens",
    )(ints, new, pages)


def settle_kernel(low, pages_ref, cache_in, cache_ref, box, sems):
    count = pages_ref.shape[1]
    loads = [pltpu.make_async_copy(pages_ref.at[r], box.at[r], sems.at[0, r]) for r in range(SLOTS)]
    stores = [pltpu.make_async_copy(box.at[r], cache_ref.at[r, pl.ds(low, count), :, 0], sems.at[1, r]) for r in range(SLOTS)]
    for load in loads:
        load.start()
    for load, store in zip(loads, stores):
        load.wait()
        store.start()
    for store in stores:
        store.wait()


def settle(low, pages, cache):
    return pl.pallas_call(
        functools.partial(settle_kernel, low),
        out_shape=jax.ShapeDtypeStruct(cache.shape, cache.dtype),
        in_specs=[ANY, ANY],
        out_specs=ANY,
        scratch_shapes=[pltpu.VMEM(pages.shape, pages.dtype), pltpu.SemaphoreType.DMA((2, SLOTS))],
        input_output_aliases={1: 0},
        compiler_params=params(44),
        cost_estimate=cost(0, 2 * pages.size * 2),
        name="settle",
    )(pages, cache)


def exchange(array):
    return lax.all_to_all(array, "grp", split_axis=0, concat_axis=0, tiled=True)


def per_device(prompt_len, request_owner, page_table, kv_pool, step_input, norm_gain, w_qkv, w_out):
    width = step_input.shape[2]
    heads = w_out.shape[1] // HD
    blocks = w_qkv.shape[2] // HD
    ints = jnp.concatenate([request_owner.reshape(-1), prompt_len, page_table.reshape(-1)])

    partial = project(step_input, norm_gain.reshape(1, width), w_qkv.reshape(width, blocks * HD), request_owner.shape[0])
    near, far = [gather_pages(low, high, ints, kv_pool) for low, high in zip(CUTS, CUTS[1:])]
    sums = exchange(partial)
    near = exchange(lax.optimization_barrier((near, sums))[0])
    mine, new = attend(ints, sums, kv_pool)
    far = write_tokens(CUTS[1], ints, new, far)
    mine, far = lax.optimization_barrier((mine, far))
    line = steps_back(mine, 1, 0)
    pieces = steps_back(jnp.stack(line[:2]), 0, 1) + steps_back(jnp.stack(line[2:]), 0, 1)
    far = exchange(lax.optimization_barrier((far, pieces))[0])
    rows = arrange(pieces)

    parts = output_rows(rows, w_out.reshape(heads * HD, width))
    distances = [divmod(i, CORES) for i in range(SIDE * CORES)]
    own = total_rows([parts[0]] + [move_part(parts[i], *distances[i]) for i in range(1, len(parts))])
    attn_out = order_rows([own] + [move_part(own, *d) for d in distances[1:]])

    cache = settle(CUTS[1], far, insert(CUTS[0], ints, rows, near))
    return (attn_out, cache)


def solution(mesh):
    placed = (
        P(),
        P(),
        P("grp", None),
        P("grp", None, "tp", None, None),
        P(None, None, "grp"),
        P("grp"),
        P("grp", "tp", None),
        P("tp", None, "grp"),
    )
    return jax.shard_map(
        per_device,
        mesh=mesh,
        in_specs=placed,
        out_specs=(P(None, None, "grp"), P("grp", None, None, "tp", None, None)),
        check_vma=False,
    )
```
